32 devices in a mesh: pb: 4 (over z), pa: 8 (over y, x, core).
Axes of the slice: x: 2, y: 2, z: 4, core: 2. Of those that a mesh axis runs over, the one named last changes fastest.
Arguments:
- queries: bfloat16 [8192, 1024], P('pb'), may hold values from -16 to 16
- passages: bfloat16 [16384, 1024], P('pa'), may hold values from -5 to 5
- teacher: float32 [8192, 4096], P('pb', 'pa'), may hold values from -20 to 300
- block_ids: int32 [64, 32], P('pb', 'pa'), may hold values from 0 to 127, as said below
Outputs:
- loss: float32 [8192], P(('pb', 'pa'))
- grad_queries: float32 [8192, 1024], P(('pb', 'pa'))
- grad_passages: float32 [16384, 1024], P(('pa', 'pb'))
The draws below stay inside these ranges and needn't reach their ends.
Inputs may be any that keep to these rules, and one draw needn't show every extreme that they name: Block g belongs to passage shard g // 16. Among the 64 entries of one device's tile of block_ids (rows of one index of pb, columns of one index of pa), at most 16 name blocks of one shard, and in every tile some shard is named exactly 16 times. The 4 entries of one row of a tile name blocks of different shards.
All inputs are finite; a program needn't handle non-finite values.
Results may differ from the reference program's by a relative error of at most 0.0024.
Values sent between devices are 32-bit elements; how exact they have to be, the bound alone decides.
A program may use at most 192 MiB of HBM per device.

```python
import math
import jax
import jax.numpy as jnp
from jax import lax

D = 1024
BLOCK = 128
QBLOCKS_DEV = 16
PBLOCKS_DEV = 16
SLOTS_DEV = 4
QBLOCKS = 64
PBLOCKS = 128
QUERIES = 8192
PASSAGES = 16384
SLOTS = 32


def draw_queries(key, part):
    values = jnp.clip(jax.random.normal(jax.random.fold_in(key, 1), (QUERIES, D), jnp.float32), -5.0, 5.0)
    return values.astype(jnp.bfloat16)


def draw_passages(key, part):
    values = jnp.clip(jax.random.normal(jax.random.fold_in(key, 11), (PASSAGES, D), jnp.float32), -5.0, 5.0)
    return values.astype(jnp.bfloat16)


def draw_teacher(key, part):
    heavy = (jax.random.uniform(jax.random.fold_in(key, 24), (QUERIES, SLOTS * BLOCK), jnp.float32) < 0.3).astype(jnp.float32)
    rough = jnp.clip(0.5 * jax.random.normal(jax.random.fold_in(key, 21), (QUERIES, SLOTS * BLOCK), jnp.float32), -2.0, 2.0)
    values = 3.0 * heavy + rough
    return values


def draw_block_ids(key, part):
    pa_count = SLOTS // SLOTS_DEV
    pb_count = QBLOCKS // QBLOCKS_DEV
    entries = QBLOCKS_DEV * SLOTS_DEV
    capacity = 2 * ((entries + pa_count - 1) // pa_count)
    active = entries // capacity

    def one_tile(tile_key):
        owners = jax.random.permutation(jax.random.fold_in(tile_key, 1), pa_count)
        picked = owners[jnp.arange(entries) % active]
        local_block = jax.random.randint(jax.random.fold_in(tile_key, 2), (entries,), 0, PBLOCKS_DEV)
        return (picked * PBLOCKS_DEV + local_block).reshape(QBLOCKS_DEV, SLOTS_DEV)
    tile_keys = jax.random.split(jax.random.fold_in(key, 7), pb_count * pa_count)
    all_tiles = jax.vmap(one_tile)(tile_keys).reshape(pb_count, pa_count, QBLOCKS_DEV, SLOTS_DEV)
    return all_tiles.transpose(0, 2, 1, 3).reshape(QBLOCKS, SLOTS).astype(jnp.int32)


def setup_inputs(seed: int = 0) -> dict:
    key_list = jax.random.split(jax.random.key(seed), 5)
    queries = draw_queries(jax.random.fold_in(key_list[4], 71), 0)
    passages = draw_passages(jax.random.fold_in(key_list[4], 71), 0)
    teacher = draw_teacher(jax.random.fold_in(key_list[4], 71), 0)
    block_ids = draw_block_ids(jax.random.fold_in(key_list[4], 71), 0)
    return dict(queries=queries, passages=passages, teacher=teacher, block_ids=block_ids)


loss_scale = 1024.0

def reference(queries, passages, teacher, block_ids):
    score_scale = 2.0 / math.sqrt(D)
    teacher_max = lax.optimization_barrier(jnp.max(teacher, axis=1))
    lse_teacher = teacher_max + jnp.log(lax.optimization_barrier(jnp.sum(jnp.exp(teacher - teacher_max[:, None]), axis=1)))
    teacher_probs = jnp.exp(teacher - lse_teacher[:, None])

    def one_block(grad_pass, inputs):
        block_queries, block_teacher, block_probs, block_lse, block_row = inputs
        scores = lax.dot_general(block_queries, passages, (((1,), (1,)), ((), ())), preferred_element_type=jnp.float32) * score_scale
        row_max = lax.optimization_barrier(jnp.max(scores, axis=1))
        lse_student = row_max + jnp.log(lax.optimization_barrier(jnp.sum(jnp.exp(scores - row_max[:, None]), axis=1)))
        hard_weights = jnp.zeros((BLOCK, PBLOCKS, BLOCK), jnp.float32)
        hard_weights = hard_weights.at[:, block_row.astype(jnp.int32), :].add(block_probs.reshape(BLOCK, SLOTS, BLOCK))
        hard_weights = hard_weights.reshape(BLOCK, PASSAGES)
        block_loss = lse_student + lax.optimization_barrier(jnp.sum(block_probs * (block_teacher - block_lse[:, None]), axis=1)) - lax.optimization_barrier(jnp.sum(hard_weights * scores, axis=1))
        dscore = ((jnp.exp(scores - lse_student[:, None]) - hard_weights) * (loss_scale * score_scale)).astype(jnp.bfloat16)
        grad_query = jnp.dot(dscore, passages, preferred_element_type=jnp.float32)
        grad_pass = grad_pass + lax.dot_general(dscore, block_queries, (((0,), (0,)), ((), ())), preferred_element_type=jnp.float32)
        return (grad_pass, (block_loss, grad_query))
    scan_inputs = (queries.reshape(QBLOCKS, BLOCK, D), teacher.reshape(QBLOCKS, BLOCK, SLOTS * BLOCK), teacher_probs.reshape(QBLOCKS, BLOCK, SLOTS * BLOCK), lse_teacher.reshape(QBLOCKS, BLOCK), block_ids)
    grad_pass, (all_loss, grad_query) = lax.scan(one_block, jnp.zeros((PASSAGES, D), jnp.float32), scan_inputs)
    return (all_loss.reshape(QUERIES), grad_query.reshape(QUERIES, D), grad_pass)
```

```python
import functools
import math

import jax
import jax.numpy as jnp
from jax import lax
from jax.experimental import pallas as pl
from jax.experimental.pallas import tpu as pltpu
from jax.sharding import PartitionSpec as P

BLOCK = 128
ROWS = 256
MIB = 1024 * 1024
loss_scale = 1024.0


def rows_to_lanes(columns, rows):
    lane = lax.broadcasted_iota(jnp.int32, (rows, BLOCK), 1)
    wide = jnp.zeros((rows, BLOCK), jnp.float32)
    for i, column in enumerate(columns):
        wide = jnp.where(lane == i, column, wide)
    return wide.T[0:8, :]


def pack_kernel(pick_ref, teacher_ref, tiles_ref, stats_ref):
    step = pl.program_id(0)
    rows = teacher_ref.shape[0]
    pa_count = tiles_ref.shape[0]
    for half in range(rows // BLOCK):
        block = step * (rows // BLOCK) + half
        for owner in range(pa_count):
            first = pl.multiple_of(pick_ref[owner, block] * BLOCK, BLOCK)
            tiles_ref[owner, half] = teacher_ref[
                half * BLOCK : (half + 1) * BLOCK, pl.ds(first, BLOCK)
            ]
    values = teacher_ref[...]
    top = jnp.max(values, axis=1, keepdims=True)
    below = values - top
    grown = jnp.exp(below)
    total = jnp.sum(grown, axis=1, keepdims=True)
    moment = jnp.sum(grown * below, axis=1, keepdims=True)
    stats_ref[...] = rows_to_lanes((top, total, moment), rows)


def pack(teacher, pick):
    query_count, width = teacher.shape
    pa_count, qblocks = pick.shape
    return pl.pallas_call(
        pack_kernel,
        grid_spec=pltpu.PrefetchScalarGridSpec(
            num_scalar_prefetch=1,
            grid=(query_count // ROWS,),
            in_specs=[pl.BlockSpec((ROWS, width), lambda i, pick: (i, 0))],
            out_specs=[
                pl.BlockSpec(
                    (pa_count, ROWS // BLOCK, BLOCK, BLOCK), lambda i, pick: (0, i, 0, 0)
                ),
                pl.BlockSpec((8, ROWS), lambda i, pick: (0, i)),
            ],
        ),
        out_shape=[
            jax.ShapeDtypeStruct((pa_count, qblocks, BLOCK, BLOCK), jnp.float32),
            jax.ShapeDtypeStruct((8, query_count), jnp.float32),
        ],
        compiler_params=pltpu.CompilerParams(vmem_limit_bytes=40 * MIB),
        cost_estimate=pl.CostEstimate(
            flops=6 * teacher.size,
            bytes_accessed=4 * (teacher.size + pa_count * qblocks * BLOCK * BLOCK),
            transcendentals=teacher.size,
        ),
        name="pack",
    )(pick, teacher)


def scores_kernel(score_scale, queries_ref, passages_ref, scores_ref, stats_ref):
    scores = (
        lax.dot_general(
            queries_ref[...],
            passages_ref[...],
            (((1,), (1,)), ((), ())),
            preferred_element_type=jnp.float32,
        )
        * score_scale
    )
    scores_ref[...] = scores
    top = jnp.max(scores, axis=1, keepdims=True)
    total = jnp.sum(jnp.exp(scores - top), axis=1, keepdims=True)
    stats_ref[...] = rows_to_lanes((top, total), scores.shape[0])


def score_stats(queries, passages, score_scale):
    query_count, depth = queries.shape
    passage_count = passages.shape[0]
    return pl.pallas_call(
        functools.partial(scores_kernel, score_scale),
        grid=(query_count // ROWS,),
        in_specs=[
            pl.BlockSpec((ROWS, depth), lambda i: (i, 0)),
            pl.BlockSpec((passage_count, depth), lambda i: (0, 0)),
        ],
        out_specs=[
            pl.BlockSpec((ROWS, passage_count), lambda i: (i, 0)),
            pl.BlockSpec((8, ROWS), lambda i: (0, i)),
        ],
        out_shape=[
            jax.ShapeDtypeStruct((query_count, passage_count), jnp.float32),
            jax.ShapeDtypeStruct((8, query_count), jnp.float32),
        ],
        compiler_params=pltpu.CompilerParams(vmem_limit_bytes=40 * MIB),
        cost_estimate=pl.CostEstimate(
            flops=2 * query_count * passage_count * depth,
            bytes_accessed=4 * query_count * passage_count
            + 2 * depth * (query_count + passage_count),
            transcendentals=query_count * passage_count,
        ),
        name="score_stats",
    )(queries, passages)


def dscore_kernel(
    scale, col_ref, scores_ref, lse_ref, tiles_ref, passages_ref, dscore_ref, part_ref, weights
):
    step = pl.program_id(0)
    rows, passage_count = scores_ref.shape
    pa_count = tiles_ref.shape[0]
    chunks, chunk_rows, depth = part_ref.shape
    chunk_rows -= 8
    weights[...] = scale * jnp.exp(scores_ref[...] - lse_ref[:, 0:1])
    hard_parts = []
    for half in range(rows // BLOCK):
        block = step * (rows // BLOCK) + half
        span = slice(half * BLOCK, (half + 1) * BLOCK)
        lse_teacher = lse_ref[span, 1:2]

        def one_source(source, hard):
            col = col_ref[source, block]
            first = pl.multiple_of(jnp.maximum(col, 0) * BLOCK, BLOCK)
            probs = jnp.exp(tiles_ref[source, half] - lse_teacher)
            probs = jnp.where(col >= 0, probs, 0.0)
            place = pl.ds(first, BLOCK)
            weights[span, place] -= scale * probs
            return hard + probs * scores_ref[span, place]

        hard_parts.append(
            jnp.sum(
                lax.fori_loop(
                    0, pa_count, one_source, jnp.zeros((BLOCK, BLOCK), jnp.float32)
                ),
                axis=1,
                keepdims=True,
            )
        )
    hard = rows_to_lanes((jnp.concatenate(hard_parts, axis=0),), rows)
    dscore = weights[...].astype(jnp.bfloat16)
    for m in range(passage_count // BLOCK):
        dscore_ref[m] = dscore[:, m * BLOCK : (m + 1) * BLOCK]
    part = jnp.dot(dscore, passages_ref[...], preferred_element_type=jnp.float32)
    for chunk in range(chunks):
        part_ref[chunk, 0:chunk_rows, :] = part[chunk * chunk_rows : (chunk + 1) * chunk_rows]
        part_ref[chunk, chunk_rows : chunk_rows + 8, :] = jnp.zeros((8, depth), jnp.float32)
        part_ref[chunk, chunk_rows : chunk_rows + 8, 0:rows] = hard


def dscore_and_query_part(scores, lse, tiles, cols, passages, scale):
    query_count, passage_count = scores.shape
    depth = passages.shape[1]
    pa_count, qblocks = cols.shape
    chunk_rows = query_count // pa_count
    chunks = ROWS // chunk_rows
    pblocks = passage_count // BLOCK
    return pl.pallas_call(
        functools.partial(dscore_kernel, scale),
        grid_spec=pltpu.PrefetchScalarGridSpec(
            num_scalar_prefetch=1,
            grid=(query_count // ROWS,),
            in_specs=[
                pl.BlockSpec((ROWS, passage_count), lambda i, cols: (i, 0)),
                pl.BlockSpec((ROWS, 2), lambda i, cols: (i, 0)),
                pl.BlockSpec(
                    (pa_count, ROWS // BLOCK, BLOCK, BLOCK), lambda i, cols: (0, i, 0, 0)
                ),
                pl.BlockSpec((passage_count, depth), lambda i, cols: (0, 0)),
            ],
            out_specs=[
                pl.BlockSpec((pblocks, ROWS, BLOCK), lambda i, cols: (0, i, 0)),
                pl.BlockSpec((chunks, chunk_rows + 8, depth), lambda i, cols: (i, 0, 0)),
            ],
            scratch_shapes=[pltpu.VMEM((ROWS, passage_count), jnp.float32)],
        ),
        out_shape=[
            jax.ShapeDtypeStruct((pblocks, query_count, BLOCK), jnp.bfloat16),
            jax.ShapeDtypeStruct((pa_count, chunk_rows + 8, depth), jnp.float32),
        ],
        compiler_params=pltpu.CompilerParams(vmem_limit_bytes=48 * MIB),
        cost_estimate=pl.CostEstimate(
            flops=2 * query_count * passage_count * depth,
            bytes_accessed=6 * query_count * passage_count + 4 * query_count * depth,
            transcendentals=query_count * passage_count,
        ),
        name="dscore",
    )(cols, scores, lse, tiles, passages)


def passages_kernel(
    count,
    dscore_hbm,
    queries_hbm,
    out_ref,
    dscore,
    queries,
    acc,
    from_below,
    from_above,
    load_sem,
    queries_sem,
    up_send,
    up_recv,
    down_send,
    down_recv,
):
    me = lax.axis_index("pb")
    blocks = dscore.shape[0]
    share = blocks // count
    low = me < count // 2

    def in_order(k):
        return jnp.where(low, blocks - 1 - k, k)

    def load(m):
        return pltpu.make_async_copy(dscore_hbm.at[m], dscore.at[m], load_sem.at[m])

    load_queries = pltpu.make_async_copy(queries_hbm, queries, queries_sem)
    load_queries.start()

    @pl.loop(0, blocks)
    def _(k):
        load(in_order(k)).start()

    barrier = pltpu.get_barrier_semaphore()

    @pl.when(me > 0)
    def _():
        pl.semaphore_signal(
            barrier, inc=1, device_id={"pb": me - 1}, device_id_type=pl.DeviceIdType.MESH
        )

    @pl.when(me < count - 1)
    def _():
        pl.semaphore_signal(
            barrier, inc=1, device_id={"pb": me + 1}, device_id_type=pl.DeviceIdType.MESH
        )

    pl.semaphore_wait(
        barrier, jnp.where(me > 0, 1, 0) + jnp.where(me < count - 1, 1, 0)
    )

    def up(m):
        return pltpu.make_async_remote_copy(
            src_ref=acc.at[m],
            dst_ref=from_below.at[m],
            send_sem=up_send.at[m],
            recv_sem=up_recv.at[m],
            device_id={"pb": me + 1},
            device_id_type=pl.DeviceIdType.MESH,
        )

    def down(m):
        return pltpu.make_async_remote_copy(
            src_ref=acc.at[m],
            dst_ref=from_above.at[m],
            send_sem=down_send.at[m],
            recv_sem=down_recv.at[m],
            device_id={"pb": me - 1},
            device_id_type=pl.DeviceIdType.MESH,
        )

    load_queries.wait()

    @pl.loop(0, blocks)
    def _(k):
        m = in_order(k)
        load(m).wait()
        acc[m] = lax.dot_general(
            dscore[m],
            queries[...],
            (((0,), (0,)), ((), ())),
            preferred_element_type=jnp.float32,
        )

        @pl.when((me == 0) & (m // share > me))
        def _():
            up(m).start()

        @pl.when((me == count - 1) & (m // share < me))
        def _():
            down(m).start()

    @pl.loop(0, blocks)
    def _(k):
        upper = blocks - 1 - k

        @pl.when((me > 0) & (upper // share >= me))
        def _():
            up(upper).wait_recv()
            acc[upper] += from_below[upper]

            @pl.when(upper // share > me)
            def _():
                up(upper).start()

        @pl.when((me < count - 1) & (k // share <= me))
        def _():
            down(k).wait_recv()
            acc[k] += from_above[k]

            @pl.when(k // share < me)
            def _():
                down(k).start()

    for c in range(share):
        out_ref[c * BLOCK : (c + 1) * BLOCK, :] = acc[me * share + c]

    @pl.loop(0, blocks)
    def _(m):
        @pl.when(m // share > me)
        def _():
            up(m).wait_send()

        @pl.when(m // share < me)
        def _():
            down(m).wait_send()


def passage_gradient(dscore, queries, count):
    blocks, query_count, _ = dscore.shape
    depth = queries.shape[1]
    rows = blocks // count * BLOCK
    return pl.pallas_call(
        functools.partial(passages_kernel, count),
        in_specs=[pl.BlockSpec(memory_space=pl.ANY)] * 2,
        out_specs=pl.BlockSpec(memory_space=pltpu.VMEM),
        out_shape=jax.ShapeDtypeStruct((rows, depth), jnp.float32),
        scratch_shapes=[
            pltpu.VMEM((blocks, query_count, BLOCK), jnp.bfloat16),
            pltpu.VMEM((query_count, depth), jnp.bfloat16),
            pltpu.VMEM((blocks, BLOCK, depth), jnp.float32),
            pltpu.VMEM((blocks, BLOCK, depth), jnp.float32),
            pltpu.VMEM((blocks, BLOCK, depth), jnp.float32),
            pltpu.SemaphoreType.DMA((blocks,)),
            pltpu.SemaphoreType.DMA,
            pltpu.SemaphoreType.DMA((blocks,)),
            pltpu.SemaphoreType.DMA((blocks,)),
            pltpu.SemaphoreType.DMA((blocks,)),
            pltpu.SemaphoreType.DMA((blocks,)),
        ],
        compiler_params=pltpu.CompilerParams(
            collective_id=0, has_side_effects=True, vmem_limit_bytes=48 * MIB
        ),
        cost_estimate=pl.CostEstimate(
            flops=2 * query_count * blocks * BLOCK * depth,
            bytes_accessed=200 * MIB,
            transcendentals=0,
        ),
        name="passage_gradient",
    )(dscore, queries)


def per_device(queries, passages, teacher, block_ids):
    query_count, depth = queries.shape
    passage_count = passages.shape[0]
    qblocks, slots = block_ids.shape
    pblocks = passage_count // BLOCK
    pa_count = lax.axis_size("pa")
    pb_count = lax.axis_size("pb")
    me = lax.axis_index("pa")
    score_scale = 2.0 / math.sqrt(depth)

    owners = block_ids // pblocks
    shard = jnp.arange(pa_count, dtype=jnp.int32)
    pick = jnp.sum(
        jnp.where(
            owners[None] == shard[:, None, None], jnp.arange(slots, dtype=jnp.int32), 0
        ),
        axis=2,
    )
    packed, teacher_stats = pack(teacher, pick)
    tiles = lax.all_to_all(packed, "pa", split_axis=0, concat_axis=0, tiled=True)

    scores, student_stats = score_stats(queries, passages, score_scale)
    entries = qblocks * slots
    ids = jnp.pad(
        block_ids.astype(jnp.float32).reshape(1, entries), ((0, 0), (0, query_count - entries))
    )
    mine = jnp.concatenate([student_stats[0:2], teacher_stats[0:3], ids], axis=0)
    every = lax.all_gather(mine, "pa")
    top, total, teacher_top, teacher_total, moment = (every[:, i] for i in range(5))
    whole_top = jnp.max(top, axis=0)
    lse_student = whole_top + jnp.log(jnp.sum(total * jnp.exp(top - whole_top), axis=0))
    whole_teacher = jnp.max(teacher_top, axis=0)
    lse_teacher = whole_teacher + jnp.log(
        jnp.sum(teacher_total * jnp.exp(teacher_top - whole_teacher), axis=0)
    )
    below = teacher_top - lse_teacher
    teacher_part = jnp.sum(jnp.exp(below) * (moment + below * teacher_total), axis=0)
    every_ids = every[:, 5, 0:entries].astype(jnp.int32).reshape(pa_count, qblocks, slots)
    cols = (
        jnp.sum(
            jnp.where(every_ids // pblocks == me, every_ids % pblocks + 1, 0), axis=2
        )
        - 1
    )
    lse = jnp.stack([lse_student, lse_teacher], axis=1)

    dscore, query_part = dscore_and_query_part(
        scores, lse, tiles, cols, passages, loss_scale * score_scale
    )
    summed = lax.psum_scatter(query_part, "pa", scatter_dimension=0, tiled=False)
    grad_passages = passage_gradient(dscore, queries, pb_count)
    row_count = query_count // pa_count
    grad_queries = summed[0:row_count]
    hard = lax.dynamic_slice_in_dim(
        summed[row_count], me * row_count % ROWS, row_count
    )
    loss_rows = (
        lax.dynamic_slice_in_dim(lse_student + teacher_part, me * row_count, row_count) - hard
    )
    return (loss_rows, grad_queries, grad_passages)


def solution(mesh):
    in_specs = (P("pb", None), P("pa", None), P("pb", "pa"), P("pb", "pa"))
    out_specs = (P(("pb", "pa")), P(("pb", "pa"), None), P(("pa", "pb"), None))
    return jax.shard_map(
        per_device, mesh=mesh, in_specs=in_specs, out_specs=out_specs, check_vma=False
    )
```

```python
import functools
import math

import jax
import jax.numpy as jnp
from jax import lax
from jax.experimental import pallas as pl
from jax.experimental.pallas import tpu as pltpu
from jax.sharding import PartitionSpec as P

BLOCK = 128
ROWS = 256
MIB = 1024 * 1024
loss_scale = 1024.0


def rows_to_lanes(columns, rows):
    lane = lax.broadcasted_iota(jnp.int32, (rows, BLOCK), 1)
    wide = jnp.zeros((rows, BLOCK), jnp.float32)
    for i, column in enumerate(columns):
        wide = jnp.where(lane == i, column, wide)
    return wide.T[0:8, :]


def pack_kernel(pick_ref, teacher_ref, tiles_ref, stats_ref):
    step = pl.program_id(0)
    rows = teacher_ref.shape[0]
    pa_count = tiles_ref.shape[0]
    for half in range(rows // BLOCK):
        block = step * (rows // BLOCK) + half
        for owner in range(pa_count):
            first = pl.multiple_of(pick_ref[owner, block] * BLOCK, BLOCK)
            tiles_ref[owner, half] = teacher_ref[
                half * BLOCK : (half + 1) * BLOCK, pl.ds(first, BLOCK)
            ]
    values = teacher_ref[...]
    top = jnp.max(values, axis=1, keepdims=True)
    below = values - top
    grown = jnp.exp(below)
    total = jnp.sum(grown, axis=1, keepdims=True)
    moment = jnp.sum(grown * below, axis=1, keepdims=True)
    stats_ref[...] = rows_to_lanes((top, total, moment), rows)


def pack(teacher, pick):
    query_count, width = teacher.shape
    pa_count, qblocks = pick.shape
    return pl.pallas_call(
        pack_kernel,
        grid_spec=pltpu.PrefetchScalarGridSpec(
            num_scalar_prefetch=1,
            grid=(query_count // ROWS,),
            in_specs=[pl.BlockSpec((ROWS, width), lambda i, pick: (i, 0))],
            out_specs=[
                pl.BlockSpec(
                    (pa_count, ROWS // BLOCK, BLOCK, BLOCK), lambda i, pick: (0, i, 0, 0)
                ),
                pl.BlockSpec((8, ROWS), lambda i, pick: (0, i)),
            ],
        ),
        out_shape=[
            jax.ShapeDtypeStruct((pa_count, qblocks, BLOCK, BLOCK), jnp.float32),
            jax.ShapeDtypeStruct((8, query_count), jnp.float32),
        ],
        compiler_params=pltpu.CompilerParams(vmem_limit_bytes=56 * MIB),
        cost_estimate=pl.CostEstimate(
            flops=6 * teacher.size,
            bytes_accessed=4 * (teacher.size + pa_count * qblocks * BLOCK * BLOCK),
            transcendentals=teacher.size,
        ),
        name="pack",
    )(pick, teacher)


def scores_kernel(score_scale, queries_ref, passages_ref, scores_ref, stats_ref):
    scores = (
        lax.dot_general(
            queries_ref[...],
            passages_ref[...],
            (((1,), (1,)), ((), ())),
            preferred_element_type=jnp.float32,
        )
        * score_scale
    )
    scores_ref[...] = scores
    top = jnp.max(scores, axis=1, keepdims=True)
    total = jnp.sum(jnp.exp(scores - top), axis=1, keepdims=True)
    stats_ref[...] = rows_to_lanes((top, total), scores.shape[0])


def score_stats(queries, passages, score_scale):
    query_count, depth = queries.shape
    passage_count = passages.shape[0]
    return pl.pallas_call(
        functools.partial(scores_kernel, score_scale),
        grid=(query_count // ROWS,),
        in_specs=[
            pl.BlockSpec((ROWS, depth), lambda i: (i, 0)),
            pl.BlockSpec((passage_count, depth), lambda i: (0, 0)),
        ],
        out_specs=[
            pl.BlockSpec((ROWS, passage_count), lambda i: (i, 0)),
            pl.BlockSpec((8, ROWS), lambda i: (0, i)),
        ],
        out_shape=[
            jax.ShapeDtypeStruct((query_count, passage_count), jnp.float32),
            jax.ShapeDtypeStruct((8, query_count), jnp.float32),
        ],
        compiler_params=pltpu.CompilerParams(vmem_limit_bytes=56 * MIB),
        cost_estimate=pl.CostEstimate(
            flops=2 * query_count * passage_count * depth,
            bytes_accessed=4 * query_count * passage_count
            + 2 * depth * (query_count + passage_count),
            transcendentals=query_count * passage_count,
        ),
        name="score_stats",
    )(queries, passages)


def dscore_kernel(
    scale, col_ref, scores_ref, lse_ref, tiles_ref, passages_ref, dscore_ref, part_ref, weights
):
    step = pl.program_id(0)
    rows, passage_count = scores_ref.shape
    pa_count = tiles_ref.shape[0]
    chunks, chunk_rows, depth = part_ref.shape
    chunk_rows -= 8
    weights[...] = scale * jnp.exp(scores_ref[...] - lse_ref[:, 0:1])
    hard_parts = []
    for half in range(rows // BLOCK):
        block = step * (rows // BLOCK) + half
        span = slice(half * BLOCK, (half + 1) * BLOCK)
        lse_teacher = lse_ref[span, 1:2]

        def one_source(source, hard):
            col = col_ref[source, block]
            first = pl.multiple_of(jnp.maximum(col, 0) * BLOCK, BLOCK)
            probs = jnp.exp(tiles_ref[source, half] - lse_teacher)
            probs = jnp.where(col >= 0, probs, 0.0)
            place = pl.ds(first, BLOCK)
            weights[span, place] -= scale * probs
            return hard + probs * scores_ref[span, place]

        hard_parts.append(
            jnp.sum(
                lax.fori_loop(
                    0,
                    pa_count,
                    one_source,
                    jnp.zeros((BLOCK, BLOCK), jnp.float32),
                    unroll=4,
                ),
                axis=1,
                keepdims=True,
            )
        )
    hard = rows_to_lanes((jnp.concatenate(hard_parts, axis=0),), rows)
    dscore = weights[...].astype(jnp.bfloat16)
    for m in range(passage_count // BLOCK):
        dscore_ref[m] = dscore[:, m * BLOCK : (m + 1) * BLOCK]
    part = jnp.dot(dscore, passages_ref[...], preferred_element_type=jnp.float32)
    for chunk in range(chunks):
        part_ref[chunk, 0:chunk_rows, :] = part[chunk * chunk_rows : (chunk + 1) * chunk_rows]
        part_ref[chunk, chunk_rows : chunk_rows + 8, :] = jnp.zeros((8, depth), jnp.float32)
        part_ref[chunk, chunk_rows : chunk_rows + 8, 0:rows] = hard


def dscore_and_query_part(scores, lse, tiles, cols, passages, scale):
    query_count, passage_count = scores.shape
    depth = passages.shape[1]
    pa_count, qblocks = cols.shape
    chunk_rows = query_count // pa_count
    chunks = ROWS // chunk_rows
    pblocks = passage_count // BLOCK
    return pl.pallas_call(
        functools.partial(dscore_kernel, scale),
        grid_spec=pltpu.PrefetchScalarGridSpec(
            num_scalar_prefetch=1,
            grid=(query_count // ROWS,),
            in_specs=[
                pl.BlockSpec((ROWS, passage_count), lambda i, cols: (i, 0)),
                pl.BlockSpec((ROWS, 2), lambda i, cols: (i, 0)),
                pl.BlockSpec(
                    (pa_count, ROWS // BLOCK, BLOCK, BLOCK), lambda i, cols: (0, i, 0, 0)
                ),
                pl.BlockSpec((passage_count, depth), lambda i, cols: (0, 0)),
            ],
            out_specs=[
                pl.BlockSpec((pblocks, ROWS, BLOCK), lambda i, cols: (0, i, 0)),
                pl.BlockSpec((chunks, chunk_rows + 8, depth), lambda i, cols: (i, 0, 0)),
            ],
            scratch_shapes=[pltpu.VMEM((ROWS, passage_count), jnp.float32)],
        ),
        out_shape=[
            jax.ShapeDtypeStruct((pblocks, query_count, BLOCK), jnp.bfloat16),
            jax.ShapeDtypeStruct((pa_count, chunk_rows + 8, depth), jnp.float32),
        ],
        compiler_params=pltpu.CompilerParams(vmem_limit_bytes=56 * MIB),
        cost_estimate=pl.CostEstimate(
            flops=2 * query_count * passage_count * depth,
            bytes_accessed=6 * query_count * passage_count + 4 * query_count * depth,
            transcendentals=query_count * passage_count,
        ),
        name="dscore",
    )(cols, scores, lse, tiles, passages)


def passages_kernel(
    count,
    dscore_hbm,
    queries_hbm,
    out_ref,
    dscore,
    queries,
    acc,
    from_below,
    from_above,
    load_sem,
    queries_sem,
    up_send,
    up_recv,
    down_send,
    down_recv,
):
    me = lax.axis_index("pb")
    blocks = dscore.shape[0]
    share = blocks // count
    low = me < count // 2

    def in_order(k):
        return jnp.where(low, blocks - 1 - k, k)

    def load(m):
        return pltpu.make_async_copy(dscore_hbm.at[m], dscore.at[m], load_sem.at[m])

    load_queries = pltpu.make_async_copy(queries_hbm, queries, queries_sem)
    load_queries.start()

    @pl.loop(0, blocks)
    def _(k):
        load(in_order(k)).start()

    barrier = pltpu.get_barrier_semaphore()

    @pl.when(me > 0)
    def _():
        pl.semaphore_signal(
            barrier, inc=1, device_id={"pb": me - 1}, device_id_type=pl.DeviceIdType.MESH
        )

    @pl.when(me < count - 1)
    def _():
        pl.semaphore_signal(
            barrier, inc=1, device_id={"pb": me + 1}, device_id_type=pl.DeviceIdType.MESH
        )

    pl.semaphore_wait(
        barrier, jnp.where(me > 0, 1, 0) + jnp.where(me < count - 1, 1, 0)
    )

    def up(m):
        return pltpu.make_async_remote_copy(
            src_ref=acc.at[m],
            dst_ref=from_below.at[m],
            send_sem=up_send.at[m],
            recv_sem=up_recv.at[m],
            device_id={"pb": me + 1},
            device_id_type=pl.DeviceIdType.MESH,
        )

    def down(m):
        return pltpu.make_async_remote_copy(
            src_ref=acc.at[m],
            dst_ref=from_above.at[m],
            send_sem=down_send.at[m],
            recv_sem=down_recv.at[m],
            device_id={"pb": me - 1},
            device_id_type=pl.DeviceIdType.MESH,
        )

    load_queries.wait()

    @pl.loop(0, blocks)
    def _(k):
        m = in_order(k)
        load(m).wait()
        acc[m] = lax.dot_general(
            dscore[m],
            queries[...],
            (((0,), (0,)), ((), ())),
            preferred_element_type=jnp.float32,
        )

        @pl.when((me == 0) & (m // share > me))
        def _():
            up(m).start()

        @pl.when((me == count - 1) & (m // share < me))
        def _():
            down(m).start()

    @pl.loop(0, blocks + count - 2)
    def _(step):
        from_low = step - (me - 1)
        upper = blocks - 1 - from_low

        @pl.when((me > 0) & (from_low >= 0) & (upper // share >= me) & (upper >= 0))
        def _():
            up(upper).wait_recv()
            acc[upper] += from_below[upper]

            @pl.when(upper // share > me)
            def _():
                up(upper).start()

        lower = step - (count - 2 - me)

        @pl.when((me < count - 1) & (lower >= 0) & (lower // share <= me))
        def _():
            down(lower).wait_recv()
            acc[lower] += from_above[lower]

            @pl.when(lower // share < me)
            def _():
                down(lower).start()

    for c in range(share):
        out_ref[c * BLOCK : (c + 1) * BLOCK, :] = acc[me * share + c]

    @pl.loop(0, blocks)
    def _(m):
        @pl.when(m // share > me)
        def _():
            up(m).wait_send()

        @pl.when(m // share < me)
        def _():
            down(m).wait_send()


def passage_gradient(dscore, queries, count):
    blocks, query_count, _ = dscore.shape
    depth = queries.shape[1]
    rows = blocks // count * BLOCK
    return pl.pallas_call(
        functools.partial(passages_kernel, count),
        in_specs=[pl.BlockSpec(memory_space=pl.ANY)] * 2,
        out_specs=pl.BlockSpec(memory_space=pltpu.VMEM),
        out_shape=jax.ShapeDtypeStruct((rows, depth), jnp.float32),
        scratch_shapes=[
            pltpu.VMEM((blocks, query_count, BLOCK), jnp.bfloat16),
            pltpu.VMEM((query_count, depth), jnp.bfloat16),
            pltpu.VMEM((blocks, BLOCK, depth), jnp.float32),
            pltpu.VMEM((blocks, BLOCK, depth), jnp.float32),
            pltpu.VMEM((blocks, BLOCK, depth), jnp.float32),
            pltpu.SemaphoreType.DMA((blocks,)),
            pltpu.SemaphoreType.DMA,
            pltpu.SemaphoreType.DMA((blocks,)),
            pltpu.SemaphoreType.DMA((blocks,)),
            pltpu.SemaphoreType.DMA((blocks,)),
            pltpu.SemaphoreType.DMA((blocks,)),
        ],
        compiler_params=pltpu.CompilerParams(
            collective_id=0, has_side_effects=True, vmem_limit_bytes=56 * MIB
        ),
        cost_estimate=pl.CostEstimate(
            flops=2 * query_count * blocks * BLOCK * depth,
            bytes_accessed=200 * MIB,
            transcendentals=0,
        ),
        name="passage_gradient",
    )(dscore, queries)


def per_device(queries, passages, teacher, block_ids):
    query_count, depth = queries.shape
    passage_count = passages.shape[0]
    qblocks, slots = block_ids.shape
    pblocks = passage_count // BLOCK
    pa_count = lax.axis_size("pa")
    pb_count = lax.axis_size("pb")
    me = lax.axis_index("pa")
    score_scale = 2.0 / math.sqrt(depth)

    owners = block_ids // pblocks
    shard = jnp.arange(pa_count, dtype=jnp.int32)
    pick = jnp.sum(
        jnp.where(
            owners[None] == shard[:, None, None], jnp.arange(slots, dtype=jnp.int32), 0
        ),
        axis=2,
    )
    packed, teacher_stats = pack(teacher, pick)
    tiles = lax.all_to_all(packed, "pa", split_axis=0, concat_axis=0, tiled=True)

    scores, student_stats = score_stats(queries, passages, score_scale)
    entries = qblocks * slots
    ids = jnp.pad(
        block_ids.astype(jnp.float32).reshape(1, entries), ((0, 0), (0, query_count - entries))
    )
    mine = jnp.concatenate([student_stats[0:2], teacher_stats[0:3], ids], axis=0)
    every = lax.all_gather(mine, "pa")
    top, total, teacher_top, teacher_total, moment = (every[:, i] for i in range(5))
    whole_top = jnp.max(top, axis=0)
    lse_student = whole_top + jnp.log(jnp.sum(total * jnp.exp(top - whole_top), axis=0))
    whole_teacher = jnp.max(teacher_top, axis=0)
    lse_teacher = whole_teacher + jnp.log(
        jnp.sum(teacher_total * jnp.exp(teacher_top - whole_teacher), axis=0)
    )
    below = teacher_top - lse_teacher
    teacher_part = jnp.sum(jnp.exp(below) * (moment + below * teacher_total), axis=0)
    every_ids = every[:, 5, 0:entries].astype(jnp.int32).reshape(pa_count, qblocks, slots)
    cols = (
        jnp.sum(
            jnp.where(every_ids // pblocks == me, every_ids % pblocks + 1, 0), axis=2
        )
        - 1
    )
    lse = jnp.stack([lse_student, lse_teacher], axis=1)

    dscore, query_part = dscore_and_query_part(
        scores, lse, tiles, cols, passages, loss_scale * score_scale
    )
    summed = lax.psum_scatter(query_part, "pa", scatter_dimension=0, tiled=False)
    grad_passages = passage_gradient(dscore, queries, pb_count)
    row_count = query_count // pa_count
    grad_queries = summed[0:row_count]
    hard = lax.dynamic_slice_in_dim(
        summed[row_count], me * row_count % ROWS, row_count
    )
    loss_rows = (
        lax.dynamic_slice_in_dim(lse_student + teacher_part, me * row_count, row_count) - hard
    )
    return (loss_rows, grad_queries, grad_passages)


def solution(mesh):
    in_specs = (P("pb", None), P("pa", None), P("pb", "pa"), P("pb", "pa"))
    out_specs = (P(("pb", "pa")), P(("pb", "pa"), None), P(("pa", "pb"), None))
    return jax.shard_map(
        per_device, mesh=mesh, in_specs=in_specs, out_specs=out_specs, check_vma=False
    )
```

```python
import functools
import math

import jax
import jax.numpy as jnp
from jax import lax
from jax.experimental import pallas as pl
from jax.experimental.pallas import tpu as pltpu
from jax.sharding import PartitionSpec as P

BLOCK = 128
ROWS = 256
MIB = 1024 * 1024
loss_scale = 1024.0


def rows_to_lanes(columns, rows):
    lane = lax.broadcasted_iota(jnp.int32, (rows, BLOCK), 1)
    wide = jnp.zeros((rows, BLOCK), jnp.float32)
    for i, column in enumerate(columns):
        wide = jnp.where(lane == i, column, wide)
    return wide.T[0:8, :]


def pack_kernel(pick_ref, teacher_ref, tiles_ref, stats_ref):
    step = pl.program_id(0)
    rows = teacher_ref.shape[0]
    pa_count = tiles_ref.shape[0]
    for half in range(rows // BLOCK):
        block = step * (rows // BLOCK) + half
        for owner in range(pa_count):
            first = pl.multiple_of(pick_ref[owner, block] * BLOCK, BLOCK)
            tiles_ref[owner, half] = teacher_ref[
                half * BLOCK : (half + 1) * BLOCK, pl.ds(first, BLOCK)
            ]
    values = teacher_ref[...]
    top = jnp.max(values, axis=1, keepdims=True)
    below = values - top
    grown = jnp.exp(below)
    total = jnp.sum(grown, axis=1, keepdims=True)
    moment = jnp.sum(grown * below, axis=1, keepdims=True)
    stats_ref[...] = rows_to_lanes((top, total, moment), rows)


def pack(teacher, pick):
    query_count, width = teacher.shape
    pa_count, qblocks = pick.shape
    return pl.pallas_call(
        pack_kernel,
        grid_spec=pltpu.PrefetchScalarGridSpec(
            num_scalar_prefetch=1,
            grid=(query_count // ROWS,),
            in_specs=[pl.BlockSpec((ROWS, width), lambda i, pick: (i, 0))],
            out_specs=[
                pl.BlockSpec(
                    (pa_count, ROWS // BLOCK, BLOCK, BLOCK), lambda i, pick: (0, i, 0, 0)
                ),
                pl.BlockSpec((8, ROWS), lambda i, pick: (0, i)),
            ],
        ),
        out_shape=[
            jax.ShapeDtypeStruct((pa_count, qblocks, BLOCK, BLOCK), jnp.float32),
            jax.ShapeDtypeStruct((8, query_count), jnp.float32),
        ],
        compiler_params=pltpu.CompilerParams(vmem_limit_bytes=56 * MIB),
        cost_estimate=pl.CostEstimate(
            flops=6 * teacher.size,
            bytes_accessed=4 * (teacher.size + pa_count * qblocks * BLOCK * BLOCK),
            transcendentals=teacher.size,
        ),
        name="pack",
    )(pick, teacher)


def scores_kernel(score_scale, queries_ref, passages_ref, scores_ref, stats_ref):
    scores = (
        lax.dot_general(
            queries_ref[...],
            passages_ref[...],
            (((1,), (1,)), ((), ())),
            preferred_element_type=jnp.float32,
        )
        * score_scale
    )
    scores_ref[...] = scores
    top = jnp.max(scores, axis=1, keepdims=True)
    total = jnp.sum(jnp.exp(scores - top), axis=1, keepdims=True)
    stats_ref[...] = rows_to_lanes((top, total), scores.shape[0])


def score_stats(queries, passages, score_scale):
    query_count, depth = queries.shape
    passage_count = passages.shape[0]
    return pl.pallas_call(
        functools.partial(scores_kernel, score_scale),
        grid=(query_count // ROWS,),
        in_specs=[
            pl.BlockSpec((ROWS, depth), lambda i: (i, 0)),
            pl.BlockSpec((passage_count, depth), lambda i: (0, 0)),
        ],
        out_specs=[
            pl.BlockSpec((ROWS, passage_count), lambda i: (i, 0)),
            pl.BlockSpec((8, ROWS), lambda i: (0, i)),
        ],
        out_shape=[
            jax.ShapeDtypeStruct((query_count, passage_count), jnp.float32),
            jax.ShapeDtypeStruct((8, query_count), jnp.float32),
        ],
        compiler_params=pltpu.CompilerParams(vmem_limit_bytes=56 * MIB),
        cost_estimate=pl.CostEstimate(
            flops=2 * query_count * passage_count * depth,
            bytes_accessed=4 * query_count * passage_count
            + 2 * depth * (query_count + passage_count),
            transcendentals=query_count * passage_count,
        ),
        name="score_stats",
    )(queries, passages)


def dscore_kernel(
    scale, col_ref, scores_ref, lse_ref, tiles_ref, dscore_ref, hard_ref, weights
):
    step = pl.program_id(0)
    rows, passage_count = scores_ref.shape
    pa_count = tiles_ref.shape[0]
    weights[...] = scale * jnp.exp(scores_ref[...] - lse_ref[:, 0:1])
    hard_parts = []
    for half in range(rows // BLOCK):
        block = step * (rows // BLOCK) + half
        span = slice(half * BLOCK, (half + 1) * BLOCK)
        lse_teacher = lse_ref[span, 1:2]

        def one_source(source, hard):
            col = col_ref[source, block]
            first = pl.multiple_of(jnp.maximum(col, 0) * BLOCK, BLOCK)
            probs = jnp.exp(tiles_ref[source, half] - lse_teacher)
            probs = jnp.where(col >= 0, probs, 0.0)
            place = pl.ds(first, BLOCK)
            weights[span, place] -= scale * probs
            return hard + probs * scores_ref[span, place]

        hard_parts.append(
            jnp.sum(
                lax.fori_loop(
                    0,
                    pa_count,
                    one_source,
                    jnp.zeros((BLOCK, BLOCK), jnp.float32),
                    unroll=4,
                ),
                axis=1,
                keepdims=True,
            )
        )
    hard_ref[...] = rows_to_lanes((jnp.concatenate(hard_parts, axis=0),), rows)
    dscore_ref[...] = weights[...].astype(jnp.bfloat16)


def dscore_and_hard(scores, lse, tiles, cols, scale):
    query_count, passage_count = scores.shape
    pa_count, qblocks = cols.shape
    return pl.pallas_call(
        functools.partial(dscore_kernel, scale),
        grid_spec=pltpu.PrefetchScalarGridSpec(
            num_scalar_prefetch=1,
            grid=(query_count // ROWS,),
            in_specs=[
                pl.BlockSpec((ROWS, passage_count), lambda i, cols: (i, 0)),
                pl.BlockSpec((ROWS, 2), lambda i, cols: (i, 0)),
                pl.BlockSpec(
                    (pa_count, ROWS // BLOCK, BLOCK, BLOCK), lambda i, cols: (0, i, 0, 0)
                ),
            ],
            out_specs=[
                pl.BlockSpec((ROWS, passage_count), lambda i, cols: (i, 0)),
                pl.BlockSpec((8, ROWS), lambda i, cols: (0, i)),
            ],
            scratch_shapes=[pltpu.VMEM((ROWS, passage_count), jnp.float32)],
        ),
        out_shape=[
            jax.ShapeDtypeStruct((query_count, passage_count), jnp.bfloat16),
            jax.ShapeDtypeStruct((8, query_count), jnp.float32),
        ],
        compiler_params=pltpu.CompilerParams(vmem_limit_bytes=56 * MIB),
        cost_estimate=pl.CostEstimate(
            flops=4 * query_count * passage_count,
            bytes_accessed=8 * query_count * passage_count,
            transcendentals=query_count * passage_count,
        ),
        name="dscore",
    )(cols, scores, lse, tiles)


def gradients_kernel(
    count,
    pa_count,
    hard_ref,
    dscore_hbm,
    queries_hbm,
    passages_hbm,
    passage_out,
    query_out,
    hard_out,
    dscore,
    queries,
    passages,
    acc,
    landed,
    part,
    part_landed,
    load_sem,
    queries_sem,
    passages_sem,
    up_send,
    up_recv,
    down_send,
    down_recv,
    part_send,
    part_recv,
):
    me = lax.axis_index("pb")
    column = lax.axis_index("pa")
    blocks = acc.shape[0]
    share = blocks // count
    depth = queries.shape[1]
    rows = query_out.shape[0]
    low = me < count // 2

    def in_order(k):
        return jnp.where(low, blocks - 1 - k, k)

    def load(m):
        place = pl.ds(pl.multiple_of(m * BLOCK, BLOCK), BLOCK)
        return pltpu.make_async_copy(
            dscore_hbm.at[:, place], dscore.at[:, place], load_sem.at[m]
        )

    load_queries = pltpu.make_async_copy(queries_hbm, queries, queries_sem)
    load_queries.start()

    @pl.loop(0, blocks)
    def _(k):
        load(in_order(k)).start()

    load_passages = pltpu.make_async_copy(passages_hbm, passages, passages_sem)
    load_passages.start()

    barrier = pltpu.get_barrier_semaphore()

    @pl.when(me > 0)
    def _():
        pl.semaphore_signal(
            barrier, inc=1, device_id={"pb": me - 1}, device_id_type=pl.DeviceIdType.MESH
        )

    @pl.when(me < count - 1)
    def _():
        pl.semaphore_signal(
            barrier, inc=1, device_id={"pb": me + 1}, device_id_type=pl.DeviceIdType.MESH
        )

    @pl.loop(1, pa_count)
    def _(k):
        pl.semaphore_signal(
            barrier,
            inc=1,
            device_id={"pa": lax.rem(column + k, pa_count)},
            device_id_type=pl.DeviceIdType.MESH,
        )

    pl.semaphore_wait(
        barrier,
        pa_count - 1 + jnp.where(me > 0, 1, 0) + jnp.where(me < count - 1, 1, 0),
    )

    def up(m):
        return pltpu.make_async_remote_copy(
            src_ref=acc.at[m],
            dst_ref=landed.at[m + share],
            send_sem=up_send.at[m],
            recv_sem=up_recv.at[m],
            device_id={"pb": me + 1},
            device_id_type=pl.DeviceIdType.MESH,
        )

    def down(m):
        return pltpu.make_async_remote_copy(
            src_ref=acc.at[m],
            dst_ref=landed.at[m],
            send_sem=down_send.at[m],
            recv_sem=down_recv.at[m],
            device_id={"pb": me - 1},
            device_id_type=pl.DeviceIdType.MESH,
        )

    def share_part(target, slot):
        return pltpu.make_async_remote_copy(
            src_ref=part.at[target],
            dst_ref=part_landed.at[column],
            send_sem=part_send.at[target],
            recv_sem=part_recv.at[slot],
            device_id={"pa": target},
            device_id_type=pl.DeviceIdType.MESH,
        )

    def part_from(source):
        return pltpu.make_async_remote_copy(
            src_ref=part.at[source],
            dst_ref=part_landed.at[source],
            send_sem=part_send.at[source],
            recv_sem=part_recv.at[source],
            device_id={"pa": source},
            device_id_type=pl.DeviceIdType.MESH,
        )

    load_queries.wait()

    @pl.loop(0, blocks)
    def _(k):
        m = in_order(k)
        load(m).wait()
        acc[m] = lax.dot_general(
            dscore[:, pl.ds(pl.multiple_of(m * BLOCK, BLOCK), BLOCK)],
            queries[...],
            (((0,), (0,)), ((), ())),
            preferred_element_type=jnp.float32,
        )

        @pl.when((me == 0) & (m // share > me))
        def _():
            up(m).start()

        @pl.when((me == count - 1) & (m // share < me))
        def _():
            down(m).start()

    load_passages.wait()

    @pl.loop(1, pa_count + 1)
    def _(k):
        target = lax.rem(column + k, pa_count)
        part[target, 0:rows, :] = jnp.dot(
            dscore[pl.ds(pl.multiple_of(target * rows, rows), rows), :],
            passages[...],
            preferred_element_type=jnp.float32,
        )
        part[target, rows : rows + 8, :] = jnp.zeros((8, depth), jnp.float32)
        group = pl.multiple_of(target * rows // ROWS * ROWS, ROWS)
        part[target, rows : rows + 8, 0:ROWS] = hard_ref[:, pl.ds(group, ROWS)]

        @pl.when(k < pa_count)
        def _():
            share_part(target, column).start()

    @pl.loop(0, blocks + count - 2)
    def _(step):
        from_low = step - (me - 1)
        upper = blocks - 1 - from_low

        @pl.when((me > 0) & (from_low >= 0) & (upper // share >= me) & (upper >= 0))
        def _():
            up(upper).wait_recv()
            acc[upper] += landed[upper + share]

            @pl.when(upper // share > me)
            def _():
                up(upper).start()

        lower = step - (count - 2 - me)

        @pl.when((me < count - 1) & (lower >= 0) & (lower // share <= me))
        def _():
            down(lower).wait_recv()
            acc[lower] += landed[lower]

            @pl.when(lower // share < me)
            def _():
                down(lower).start()

    for c in range(share):
        passage_out[c * BLOCK : (c + 1) * BLOCK, :] = acc[me * share + c]

    query_out[...] = part[column, 0:rows, :]
    hard_out[...] = part[column, rows : rows + 8, 0:ROWS]

    @pl.loop(1, pa_count)
    def _(k):
        source = lax.rem(column + pa_count - k, pa_count)
        part_from(source).wait_recv()
        query_out[...] += part_landed[source, 0:rows, :]
        hard_out[...] += part_landed[source, rows : rows + 8, 0:ROWS]

    @pl.loop(1, pa_count)
    def _(k):
        target = lax.rem(column + k, pa_count)
        share_part(target, column).wait_send()

    @pl.loop(0, blocks)
    def _(m):
        @pl.when(m // share > me)
        def _():
            up(m).wait_send()

        @pl.when(m // share < me)
        def _():
            down(m).wait_send()


def gradients(hard, dscore, queries, passages, count, pa_count):
    query_count, depth = queries.shape
    passage_count = passages.shape[0]
    blocks = passage_count // BLOCK
    share = blocks // count
    rows = query_count // pa_count
    dma = pltpu.SemaphoreType.DMA
    return pl.pallas_call(
        functools.partial(gradients_kernel, count, pa_count),
        in_specs=[pl.BlockSpec(memory_space=pltpu.VMEM)]
        + [pl.BlockSpec(memory_space=pl.ANY)] * 3,
        out_specs=[pl.BlockSpec(memory_space=pltpu.VMEM)] * 3,
        out_shape=[
            jax.ShapeDtypeStruct((share * BLOCK, depth), jnp.float32),
            jax.ShapeDtypeStruct((rows, depth), jnp.float32),
            jax.ShapeDtypeStruct((8, ROWS), jnp.float32),
        ],
        scratch_shapes=[
            pltpu.VMEM((query_count, passage_count), jnp.bfloat16),
            pltpu.VMEM((query_count, depth), jnp.bfloat16),
            pltpu.VMEM((passage_count, depth), jnp.bfloat16),
            pltpu.VMEM((blocks, BLOCK, depth), jnp.float32),
            pltpu.VMEM((blocks + share, BLOCK, depth), jnp.float32),
            pltpu.VMEM((pa_count, rows + 8, depth), jnp.float32),
            pltpu.VMEM((pa_count, rows + 8, depth), jnp.float32),
            dma((blocks,)),
            dma,
            dma,
            dma((blocks,)),
            dma((blocks,)),
            dma((blocks,)),
            dma((blocks,)),
            dma((pa_count,)),
            dma((pa_count,)),
        ],
        compiler_params=pltpu.CompilerParams(
            collective_id=0, has_side_effects=True, vmem_limit_bytes=60 * MIB
        ),
        cost_estimate=pl.CostEstimate(
            flops=4 * query_count * passage_count * depth,
            bytes_accessed=200 * MIB,
            transcendentals=0,
        ),
        name="gradients",
    )(hard, dscore, queries, passages)


def per_device(queries, passages, teacher, block_ids):
    query_count, depth = queries.shape
    passage_count = passages.shape[0]
    qblocks, slots = block_ids.shape
    pblocks = passage_count // BLOCK
    pa_count = lax.axis_size("pa")
    pb_count = lax.axis_size("pb")
    me = lax.axis_index("pa")
    score_scale = 2.0 / math.sqrt(depth)

    owners = block_ids // pblocks
    shard = jnp.arange(pa_count, dtype=jnp.int32)
    pick = jnp.sum(
        jnp.where(
            owners[None] == shard[:, None, None], jnp.arange(slots, dtype=jnp.int32), 0
        ),
        axis=2,
    )
    packed, teacher_stats = pack(teacher, pick)
    tiles = lax.all_to_all(packed, "pa", split_axis=0, concat_axis=0, tiled=True)

    scores, student_stats = score_stats(queries, passages, score_scale)
    entries = qblocks * slots
    ids = jnp.pad(
        block_ids.astype(jnp.float32).reshape(1, entries), ((0, 0), (0, query_count - entries))
    )
    mine = jnp.concatenate([student_stats[0:2], teacher_stats[0:3], ids], axis=0)
    every = lax.all_gather(mine, "pa")
    top, total, teacher_top, teacher_total, moment = (every[:, i] for i in range(5))
    whole_top = jnp.max(top, axis=0)
    lse_student = whole_top + jnp.log(jnp.sum(total * jnp.exp(top - whole_top), axis=0))
    whole_teacher = jnp.max(teacher_top, axis=0)
    lse_teacher = whole_teacher + jnp.log(
        jnp.sum(teacher_total * jnp.exp(teacher_top - whole_teacher), axis=0)
    )
    below = teacher_top - lse_teacher
    teacher_part = jnp.sum(jnp.exp(below) * (moment + below * teacher_total), axis=0)
    every_ids = every[:, 5, 0:entries].astype(jnp.int32).reshape(pa_count, qblocks, slots)
    cols = (
        jnp.sum(
            jnp.where(every_ids // pblocks == me, every_ids % pblocks + 1, 0), axis=2
        )
        - 1
    )
    lse = jnp.stack([lse_student, lse_teacher], axis=1)

    dscore, hard_part = dscore_and_hard(scores, lse, tiles, cols, loss_scale * score_scale)
    grad_passages, grad_queries, hard_rows = gradients(
        hard_part, dscore, queries, passages, pb_count, pa_count
    )
    row_count = query_count // pa_count
    hard = lax.dynamic_slice_in_dim(hard_rows[0], me * row_count % ROWS, row_count)
    loss_rows = (
        lax.dynamic_slice_in_dim(lse_student + teacher_part, me * row_count, row_count) - hard
    )
    return (loss_rows, grad_queries, grad_passages)


def solution(mesh):
    in_specs = (P("pb", None), P("pa", None), P("pb", "pa"), P("pb", "pa"))
    out_specs = (P(("pb", "pa")), P(("pb", "pa"), None), P(("pa", "pb"), None))
    return jax.shard_map(
        per_device, mesh=mesh, in_specs=in_specs, out_specs=out_specs, check_vma=False
    )
```

```python
import functools
import math

import jax
import jax.numpy as jnp
from jax import lax
from jax.experimental import pallas as pl
from jax.experimental.pallas import tpu as pltpu
from jax.sharding import PartitionSpec as P

BLOCK = 128
ROWS = 256
MIB = 1024 * 1024
loss_scale = 1024.0


def rows_to_lanes(columns, rows):
    lane = lax.broadcasted_iota(jnp.int32, (rows, BLOCK), 1)
    wide = jnp.zeros((rows, BLOCK), jnp.float32)
    for i, column in enumerate(columns):
        wide = jnp.where(lane == i, column, wide)
    return wide.T[0:8, :]


def pack_kernel(pick_ref, teacher_ref, tiles_ref, stats_ref):
    step = pl.program_id(0)
    rows = teacher_ref.shape[0]
    pa_count = tiles_ref.shape[0]
    for half in range(rows // BLOCK):
        block = step * (rows // BLOCK) + half
        for owner in range(pa_count):
            first = pl.multiple_of(pick_ref[owner, block] * BLOCK, BLOCK)
            tiles_ref[owner, half] = teacher_ref[
                half * BLOCK : (half + 1) * BLOCK, pl.ds(first, BLOCK)
            ]
    values = teacher_ref[...]
    top = jnp.max(values, axis=1, keepdims=True)
    below = values - top
    grown = jnp.exp(below)
    total = jnp.sum(grown, axis=1, keepdims=True)
    moment = jnp.sum(grown * below, axis=1, keepdims=True)
    stats_ref[...] = rows_to_lanes((top, total, moment), rows)


def pack(teacher, pick):
    query_count, width = teacher.shape
    pa_count, qblocks = pick.shape
    return pl.pallas_call(
        pack_kernel,
        grid_spec=pltpu.PrefetchScalarGridSpec(
            num_scalar_prefetch=1,
            grid=(query_count // ROWS,),
            in_specs=[pl.BlockSpec((ROWS, width), lambda i, pick: (i, 0))],
            out_specs=[
                pl.BlockSpec(
                    (pa_count, ROWS // BLOCK, BLOCK, BLOCK), lambda i, pick: (0, i, 0, 0)
                ),
                pl.BlockSpec((8, ROWS), lambda i, pick: (0, i)),
            ],
        ),
        out_shape=[
            jax.ShapeDtypeStruct((pa_count, qblocks, BLOCK, BLOCK), jnp.float32),
            jax.ShapeDtypeStruct((8, query_count), jnp.float32),
        ],
        compiler_params=pltpu.CompilerParams(vmem_limit_bytes=56 * MIB),
        cost_estimate=pl.CostEstimate(
            flops=6 * teacher.size,
            bytes_accessed=4 * (teacher.size + pa_count * qblocks * BLOCK * BLOCK),
            transcendentals=teacher.size,
        ),
        name="pack",
    )(pick, teacher)


def scores_kernel(score_scale, queries_ref, passages_ref, scores_ref, stats_ref):
    scores = (
        lax.dot_general(
            queries_ref[...],
            passages_ref[...],
            (((1,), (1,)), ((), ())),
            preferred_element_type=jnp.float32,
        )
        * score_scale
    )
    scores_ref[...] = scores
    top = jnp.max(scores, axis=1, keepdims=True)
    total = jnp.sum(jnp.exp(scores - top), axis=1, keepdims=True)
    stats_ref[...] = rows_to_lanes((top, total), scores.shape[0])


def score_stats(queries, passages, score_scale):
    query_count, depth = queries.shape
    passage_count = passages.shape[0]
    return pl.pallas_call(
        functools.partial(scores_kernel, score_scale),
        grid=(query_count // ROWS,),
        in_specs=[
            pl.BlockSpec((ROWS, depth), lambda i: (i, 0)),
            pl.BlockSpec((passage_count, depth), lambda i: (0, 0)),
        ],
        out_specs=[
            pl.BlockSpec((ROWS, passage_count), lambda i: (i, 0)),
            pl.BlockSpec((8, ROWS), lambda i: (0, i)),
        ],
        out_shape=[
            jax.ShapeDtypeStruct((query_count, passage_count), jnp.float32),
            jax.ShapeDtypeStruct((8, query_count), jnp.float32),
        ],
        compiler_params=pltpu.CompilerParams(vmem_limit_bytes=56 * MIB),
        cost_estimate=pl.CostEstimate(
            flops=2 * query_count * passage_count * depth,
            bytes_accessed=4 * query_count * passage_count
            + 2 * depth * (query_count + passage_count),
            transcendentals=query_count * passage_count,
        ),
        name="score_stats",
    )(queries, passages)


def dscore_kernel(
    scale, col_ref, scores_ref, lse_ref, tiles_ref, dscore_ref, hard_ref, weights
):
    step = pl.program_id(0)
    rows, passage_count = scores_ref.shape
    pa_count = tiles_ref.shape[0]
    weights[...] = scale * jnp.exp(scores_ref[...] - lse_ref[:, 0:1])
    hard_parts = []
    for half in range(rows // BLOCK):
        block = step * (rows // BLOCK) + half
        span = slice(half * BLOCK, (half + 1) * BLOCK)
        lse_teacher = lse_ref[span, 1:2]

        def one_source(source, hard):
            col = col_ref[source, block]
            first = pl.multiple_of(jnp.maximum(col, 0) * BLOCK, BLOCK)
            probs = jnp.exp(tiles_ref[source, half] - lse_teacher)
            probs = jnp.where(col >= 0, probs, 0.0)
            place = pl.ds(first, BLOCK)
            weights[span, place] -= scale * probs
            return hard + probs * scores_ref[span, place]

        hard_parts.append(
            jnp.sum(
                lax.fori_loop(
                    0,
                    pa_count,
                    one_source,
                    jnp.zeros((BLOCK, BLOCK), jnp.float32),
                    unroll=8,
                ),
                axis=1,
                keepdims=True,
            )
        )
    hard_ref[...] = rows_to_lanes((jnp.concatenate(hard_parts, axis=0),), rows)
    dscore_ref[...] = weights[...].astype(jnp.bfloat16)


def dscore_and_hard(scores, lse, tiles, cols, scale):
    query_count, passage_count = scores.shape
    pa_count, qblocks = cols.shape
    return pl.pallas_call(
        functools.partial(dscore_kernel, scale),
        grid_spec=pltpu.PrefetchScalarGridSpec(
            num_scalar_prefetch=1,
            grid=(query_count // ROWS,),
            in_specs=[
                pl.BlockSpec((ROWS, passage_count), lambda i, cols: (i, 0)),
                pl.BlockSpec((ROWS, 2), lambda i, cols: (i, 0)),
                pl.BlockSpec(
                    (pa_count, ROWS // BLOCK, BLOCK, BLOCK), lambda i, cols: (0, i, 0, 0)
                ),
            ],
            out_specs=[
                pl.BlockSpec((ROWS, passage_count), lambda i, cols: (i, 0)),
                pl.BlockSpec((8, ROWS), lambda i, cols: (0, i)),
            ],
            scratch_shapes=[pltpu.VMEM((ROWS, passage_count), jnp.float32)],
        ),
        out_shape=[
            jax.ShapeDtypeStruct((query_count, passage_count), jnp.bfloat16),
            jax.ShapeDtypeStruct((8, query_count), jnp.float32),
        ],
        compiler_params=pltpu.CompilerParams(vmem_limit_bytes=56 * MIB),
        cost_estimate=pl.CostEstimate(
            flops=4 * query_count * passage_count,
            bytes_accessed=8 * query_count * passage_count,
            transcendentals=query_count * passage_count,
        ),
        name="dscore",
    )(cols, scores, lse, tiles)


def gradients_kernel(
    count,
    pa_count,
    hard_ref,
    dscore_hbm,
    queries_hbm,
    passages_hbm,
    passage_out,
    query_out,
    hard_out,
    dscore,
    queries,
    passages,
    acc,
    landed,
    part,
    part_landed,
    load_sem,
    queries_sem,
    passages_sem,
    up_send,
    up_recv,
    down_send,
    down_recv,
    part_send,
    part_recv,
):
    me = lax.axis_index("pb")
    column = lax.axis_index("pa")
    blocks = acc.shape[0]
    share = blocks // count
    depth = queries.shape[1]
    rows = query_out.shape[0]
    low = me < count // 2

    def in_order(k):
        return jnp.where(low, blocks - 1 - k, k)

    def load(m):
        place = pl.ds(pl.multiple_of(m * BLOCK, BLOCK), BLOCK)
        return pltpu.make_async_copy(
            dscore_hbm.at[:, place], dscore.at[:, place], load_sem.at[m]
        )

    load_queries = pltpu.make_async_copy(queries_hbm, queries, queries_sem)
    load_queries.start()

    @pl.loop(0, blocks)
    def _(k):
        load(in_order(k)).start()

    load_passages = pltpu.make_async_copy(passages_hbm, passages, passages_sem)
    load_passages.start()

    barrier = pltpu.get_barrier_semaphore()

    @pl.when(me > 0)
    def _():
        pl.semaphore_signal(
            barrier, inc=1, device_id={"pb": me - 1}, device_id_type=pl.DeviceIdType.MESH
        )

    @pl.when(me < count - 1)
    def _():
        pl.semaphore_signal(
            barrier, inc=1, device_id={"pb": me + 1}, device_id_type=pl.DeviceIdType.MESH
        )

    @pl.loop(1, pa_count)
    def _(k):
        pl.semaphore_signal(
            barrier,
            inc=1,
            device_id={"pa": lax.rem(column + k, pa_count)},
            device_id_type=pl.DeviceIdType.MESH,
        )

    pl.semaphore_wait(
        barrier,
        pa_count - 1 + jnp.where(me > 0, 1, 0) + jnp.where(me < count - 1, 1, 0),
    )

    def up(m):
        return pltpu.make_async_remote_copy(
            src_ref=acc.at[m],
            dst_ref=landed.at[m + share],
            send_sem=up_send.at[m],
            recv_sem=up_recv.at[m],
            device_id={"pb": me + 1},
            device_id_type=pl.DeviceIdType.MESH,
        )

    def down(m):
        return pltpu.make_async_remote_copy(
            src_ref=acc.at[m],
            dst_ref=landed.at[m],
            send_sem=down_send.at[m],
            recv_sem=down_recv.at[m],
            device_id={"pb": me - 1},
            device_id_type=pl.DeviceIdType.MESH,
        )

    def share_part(target, slot):
        return pltpu.make_async_remote_copy(
            src_ref=part.at[target],
            dst_ref=part_landed.at[column],
            send_sem=part_send.at[target],
            recv_sem=part_recv.at[slot],
            device_id={"pa": target},
            device_id_type=pl.DeviceIdType.MESH,
        )

    def part_from(source):
        return pltpu.make_async_remote_copy(
            src_ref=part.at[source],
            dst_ref=part_landed.at[source],
            send_sem=part_send.at[source],
            recv_sem=part_recv.at[source],
            device_id={"pa": source},
            device_id_type=pl.DeviceIdType.MESH,
        )

    load_queries.wait()

    @pl.loop(0, blocks)
    def _(k):
        m = in_order(k)
        load(m).wait()
        acc[m] = lax.dot_general(
            dscore[:, pl.ds(pl.multiple_of(m * BLOCK, BLOCK), BLOCK)],
            queries[...],
            (((0,), (0,)), ((), ())),
            preferred_element_type=jnp.float32,
        )

        @pl.when((me == 0) & (m // share > me))
        def _():
            up(m).start()

        @pl.when((me == count - 1) & (m // share < me))
        def _():
            down(m).start()

    load_passages.wait()

    @pl.loop(1, pa_count + 1)
    def _(k):
        target = lax.rem(column + k, pa_count)
        part[target, 0:rows, :] = jnp.dot(
            dscore[pl.ds(pl.multiple_of(target * rows, rows), rows), :],
            passages[...],
            preferred_element_type=jnp.float32,
        )
        part[target, rows : rows + 8, :] = jnp.zeros((8, depth), jnp.float32)
        group = pl.multiple_of(target * rows // ROWS * ROWS, ROWS)
        part[target, rows : rows + 8, 0:ROWS] = hard_ref[:, pl.ds(group, ROWS)]

        @pl.when(k < pa_count)
        def _():
            share_part(target, column).start()

    @pl.loop(0, blocks + count - 2)
    def _(step):
        from_low = step - (me - 1)
        upper = blocks - 1 - from_low

        @pl.when((me > 0) & (from_low >= 0) & (upper // share >= me) & (upper >= 0))
        def _():
            up(upper).wait_recv()
            acc[upper] += landed[upper + share]

            @pl.when(upper // share > me)
            def _():
                up(upper).start()

        lower = step - (count - 2 - me)

        @pl.when((me < count - 1) & (lower >= 0) & (lower // share <= me))
        def _():
            down(lower).wait_recv()
            acc[lower] += landed[lower]

            @pl.when(lower // share < me)
            def _():
                down(lower).start()

        @pl.when(step == max(blocks - share - 2, 0))
        def _():
            query_out[...] = part[column, 0:rows, :]
            hard_out[...] = part[column, rows : rows + 8, 0:ROWS]

            @pl.loop(1, pa_count)
            def _(k):
                source = lax.rem(column + pa_count - k, pa_count)
                part_from(source).wait_recv()
                query_out[...] += part_landed[source, 0:rows, :]
                hard_out[...] += part_landed[source, rows : rows + 8, 0:ROWS]

    for c in range(share):
        passage_out[c * BLOCK : (c + 1) * BLOCK, :] = acc[me * share + c]

    @pl.loop(1, pa_count)
    def _(k):
        target = lax.rem(column + k, pa_count)
        share_part(target, column).wait_send()

    @pl.loop(0, blocks)
    def _(m):
        @pl.when(m // share > me)
        def _():
            up(m).wait_send()

        @pl.when(m // share < me)
        def _():
            down(m).wait_send()


def gradients(hard, dscore, queries, passages, count, pa_count):
    query_count, depth = queries.shape
    passage_count = passages.shape[0]
    blocks = passage_count // BLOCK
    share = blocks // count
    rows = query_count // pa_count
    dma = pltpu.SemaphoreType.DMA
    return pl.pallas_call(
        functools.partial(gradients_kernel, count, pa_count),
        in_specs=[pl.BlockSpec(memory_space=pltpu.VMEM)]
        + [pl.BlockSpec(memory_space=pl.ANY)] * 3,
        out_specs=[pl.BlockSpec(memory_space=pltpu.VMEM)] * 3,
        out_shape=[
            jax.ShapeDtypeStruct((share * BLOCK, depth), jnp.float32),
            jax.ShapeDtypeStruct((rows, depth), jnp.float32),
            jax.ShapeDtypeStruct((8, ROWS), jnp.float32),
        ],
        scratch_shapes=[
            pltpu.VMEM((query_count, passage_count), jnp.bfloat16),
            pltpu.VMEM((query_count, depth), jnp.bfloat16),
            pltpu.VMEM((passage_count, depth), jnp.bfloat16),
            pltpu.VMEM((blocks, BLOCK, depth), jnp.float32),
            pltpu.VMEM((blocks + share, BLOCK, depth), jnp.float32),
            pltpu.VMEM((pa_count, rows + 8, depth), jnp.float32),
            pltpu.VMEM((pa_count, rows + 8, depth), jnp.float32),
            dma((blocks,)),
            dma,
            dma,
            dma((blocks,)),
            dma((blocks,)),
            dma((blocks,)),
            dma((blocks,)),
            dma((pa_count,)),
            dma((pa_count,)),
        ],
        compiler_params=pltpu.CompilerParams(
            collective_id=0, has_side_effects=True, vmem_limit_bytes=60 * MIB
        ),
        cost_estimate=pl.CostEstimate(
            flops=4 * query_count * passage_count * depth,
            bytes_accessed=200 * MIB,
            transcendentals=0,
        ),
        name="gradients",
    )(hard, dscore, queries, passages)


def per_device(queries, passages, teacher, block_ids):
    query_count, depth = queries.shape
    passage_count = passages.shape[0]
    qblocks, slots = block_ids.shape
    pblocks = passage_count // BLOCK
    pa_count = lax.axis_size("pa")
    pb_count = lax.axis_size("pb")
    me = lax.axis_index("pa")
    score_scale = 2.0 / math.sqrt(depth)

    owners = block_ids // pblocks
    shard = jnp.arange(pa_count, dtype=jnp.int32)
    pick = jnp.sum(
        jnp.where(
            owners[None] == shard[:, None, None], jnp.arange(slots, dtype=jnp.int32), 0
        ),
        axis=2,
    )
    packed, teacher_stats = pack(teacher, pick)
    tiles = lax.all_to_all(packed, "pa", split_axis=0, concat_axis=0, tiled=True)

    scores, student_stats = score_stats(queries, passages, score_scale)
    entries = qblocks * slots
    ids = jnp.pad(
        block_ids.astype(jnp.float32).reshape(1, entries), ((0, 0), (0, query_count - entries))
    )
    mine = jnp.concatenate([student_stats[0:2], teacher_stats[0:3], ids], axis=0)
    every = lax.all_gather(mine, "pa")
    top, total, teacher_top, teacher_total, moment = (every[:, i] for i in range(5))
    whole_top = jnp.max(top, axis=0)
    lse_student = whole_top + jnp.log(jnp.sum(total * jnp.exp(top - whole_top), axis=0))
    whole_teacher = jnp.max(teacher_top, axis=0)
    lse_teacher = whole_teacher + jnp.log(
        jnp.sum(teacher_total * jnp.exp(teacher_top - whole_teacher), axis=0)
    )
    below = teacher_top - lse_teacher
    teacher_part = jnp.sum(jnp.exp(below) * (moment + below * teacher_total), axis=0)
    every_ids = every[:, 5, 0:entries].astype(jnp.int32).reshape(pa_count, qblocks, slots)
    cols = (
        jnp.sum(
            jnp.where(every_ids // pblocks == me, every_ids % pblocks + 1, 0), axis=2
        )
        - 1
    )
    lse = jnp.stack([lse_student, lse_teacher], axis=1)

    dscore, hard_part = dscore_and_hard(scores, lse, tiles, cols, loss_scale * score_scale)
    grad_passages, grad_queries, hard_rows = gradients(
        hard_part, dscore, queries, passages, pb_count, pa_count
    )
    row_count = query_count // pa_count
    hard = lax.dynamic_slice_in_dim(hard_rows[0], me * row_count % ROWS, row_count)
    loss_rows = (
        lax.dynamic_slice_in_dim(lse_student + teacher_part, me * row_count, row_count) - hard
    )
    return (loss_rows, grad_queries, grad_passages)


def solution(mesh):
    in_specs = (P("pb", None), P("pa", None), P("pb", "pa"), P("pb", "pa"))
    out_specs = (P(("pb", "pa")), P(("pb", "pa"), None), P(("pa", "pb"), None))
    return jax.shard_map(
        per_device, mesh=mesh, in_specs=in_specs, out_specs=out_specs, check_vma=False
    )
```
